128 devices in a mesh: dp: 32 (over z, x_hi, y), blk: 4 (over x_lo, core).
Axes of the slice: x: 4 (x_hi: 2, x_lo: 2; x = x_hi * 2 + x_lo), y: 4, z: 4, core: 2. Of those that a mesh axis runs over, the one named last changes fastest.
Arguments:
- queries: bfloat16 [32768, 4096], P(('dp', 'blk')), may hold values from -24 to 24
- passages: bfloat16 [32768, 4096], P(('dp', 'blk')), may hold values from -16 to 16
- hard_owner: int32 [32768, 1], P(('dp', 'blk')), may hold values from 0 to 31, as said below
- hard_row: int32 [32768, 1], P(('dp', 'blk')), may hold values from 0 to 255
Outputs:
- query_embedding_gradient: float32 [32768, 4096], P(('dp', 'blk'))
- passage_grad: float32 [32768, 4096], P(('dp', 'blk'))
- loss: float32 [], replicated
The draws below stay inside these ranges and needn't reach their ends.
Inputs may be any that keep to these rules, and one draw needn't show every extreme that they name: `hard_owner`: the rows of one device name no owner more than 10 times, and one owner exactly 10 times.
All inputs are finite; a program needn't handle non-finite values.
Results may differ from the reference program's by a relative error of at most 0.0025.
Values may be sent and summed in bfloat16 or wider, within the bound.
No kernel may reach another device: no remote copies, remote signals or barrier semaphores. Data moves between devices by JAX's collectives and lax.ppermute only.
A program may use at most 128 MiB of HBM per device.

```python
import math
import jax
import jax.numpy as jnp
from jax import lax

LATENT_DIM = 4096
ROWS_DEV = 256
HARD = 1
GROUP = 1024
PAIRS = 32768
CAP = 10
N_DP = 32
N_BLK = 4


def shared_base(key):
    return jnp.clip(jax.random.normal(key, (PAIRS, LATENT_DIM), jnp.float32), -6.0, 6.0)


def mined_targets(key):
    owner_key = jax.random.fold_in(key, 401)
    offset_key = jax.random.fold_in(key, 402)
    block_count = PAIRS // ROWS_DEV
    per_block = ROWS_DEV * HARD
    pool_size = N_DP * CAP

    def one_block(block_key):
        first_key, rest_key, place_key = jax.random.split(block_key, 3)
        busiest = jax.random.randint(first_key, (), 0, N_DP)
        owner_pool = (jnp.arange(pool_size, dtype=jnp.int32) // CAP + busiest) % N_DP
        rest_part = jax.random.permutation(rest_key, owner_pool[CAP:])
        chosen_owners = jnp.concatenate([owner_pool[:CAP], rest_part])[:per_block]
        return jax.random.permutation(place_key, chosen_owners)
    block_keys = jax.random.split(owner_key, block_count)
    owners = jax.vmap(one_block)(block_keys).reshape(PAIRS, HARD).astype(jnp.int32)
    offsets = jax.random.randint(offset_key, (PAIRS, HARD), 0, ROWS_DEV).astype(jnp.int32)
    return (owners, offsets)


def target_rows(key, base_rows):
    owners, offsets = mined_targets(key)
    position = jnp.arange(PAIRS, dtype=jnp.int32)
    block_start = position // ROWS_DEV % (GROUP // ROWS_DEV) * ROWS_DEV
    targets = (owners * GROUP + block_start[:, None] + offsets).astype(jnp.int32)
    return jnp.sum(jnp.take(base_rows, targets, axis=0), axis=1)


def draw_hard_owner(key, part):
    owners, offsets = mined_targets(key)
    return owners


def draw_hard_row(key, part):
    owners, offsets = mined_targets(key)
    return offsets


def draw_passages(key, part):
    base_rows = shared_base(key)
    return base_rows.astype(jnp.bfloat16)


def draw_queries(key, part):
    base_rows = shared_base(key)
    mined_part = target_rows(key, base_rows)
    key = jax.random.fold_in(key, 23)
    jitter_key = jax.random.fold_in(key, 0)
    row_frac = jnp.arange(PAIRS, dtype=jnp.float32) / PAIRS
    jitter = jnp.clip(jax.random.normal(jitter_key, (PAIRS, LATENT_DIM), jnp.float32), -6.0, 6.0)
    row_scale = 0.7 * 3.0 ** row_frac
    return (row_scale[:, None] * (0.03 * base_rows + 0.06 * mined_part + jitter)).astype(jnp.bfloat16)


def setup_inputs(seed: int = 0) -> dict:
    key_of = jax.random.split(jax.random.key(seed), 5)
    return {
        "queries": draw_queries(jax.random.fold_in(key_of[4], 71), 0),
        "passages": draw_passages(jax.random.fold_in(key_of[4], 71), 0),
        "hard_owner": draw_hard_owner(jax.random.fold_in(key_of[4], 71), 0),
        "hard_row": draw_hard_row(jax.random.fold_in(key_of[4], 71), 0),
    }


def reference(queries, passages, hard_owner, hard_row):
    group_rows = N_BLK * ROWS_DEV
    group_count = PAIRS // group_rows
    logit_sharpness_factor = 2.0 / math.sqrt(LATENT_DIM)
    local_block = jnp.arange(group_rows, dtype=jnp.int32) // ROWS_DEV
    identity = jnp.eye(group_rows, dtype=jnp.float32)

    def per_group(hard_total, group_index):
        first_row = (group_index * group_rows).astype(jnp.int32)
        request_tile_slice = lax.dynamic_slice_in_dim(queries, first_row, group_rows, 0)
        document_tile_slice = lax.dynamic_slice_in_dim(passages, first_row, group_rows, 0)
        owners = lax.dynamic_slice_in_dim(hard_owner, first_row, group_rows, 0)
        offsets = lax.dynamic_slice_in_dim(hard_row, first_row, group_rows, 0)
        targets = (owners * group_rows + local_block[:, None] * ROWS_DEV + offsets).astype(jnp.int32)
        distractor_latent_matrix = jnp.take(passages, targets, axis=0)
        similarity_logits_within = jnp.dot(request_tile_slice, document_tile_slice.T, preferred_element_type=jnp.float32) * logit_sharpness_factor
        distractor_similarity_logits = jnp.einsum('sl,srl->sr', request_tile_slice.astype(jnp.float32), distractor_latent_matrix.astype(jnp.float32)) * logit_sharpness_factor
        row_top = jnp.maximum(lax.optimization_barrier(jnp.max(similarity_logits_within, axis=1)), lax.optimization_barrier(jnp.max(distractor_similarity_logits, axis=1)))
        row_total = lax.optimization_barrier(jnp.sum(jnp.exp(similarity_logits_within - row_top[:, None]), axis=1)) + lax.optimization_barrier(jnp.sum(jnp.exp(distractor_similarity_logits - row_top[:, None]), axis=1))
        log_norm = row_top + jnp.log(row_total)
        positive = jnp.diagonal(similarity_logits_within)
        loss_part = jnp.sum(log_norm - positive)
        inbatch_weights = (jnp.exp(similarity_logits_within - log_norm[:, None]) - identity).astype(jnp.bfloat16)
        mined_negative_weights = jnp.exp(distractor_similarity_logits - log_norm[:, None]).astype(jnp.bfloat16)
        query_embedding_gradient = jnp.dot(inbatch_weights, document_tile_slice, preferred_element_type=jnp.float32) + jnp.einsum('ro,roc->rc', mined_negative_weights.astype(jnp.float32), distractor_latent_matrix.astype(jnp.float32))
        in_grad = jnp.dot(inbatch_weights.T, request_tile_slice, preferred_element_type=jnp.float32)
        hard_terms = (mined_negative_weights.astype(jnp.float32)[:, :, None] * request_tile_slice.astype(jnp.float32)[:, None, :]).astype(jnp.bfloat16)
        hard_total = hard_total.at[targets.reshape(-1)].add(hard_terms.reshape(-1, LATENT_DIM).astype(jnp.float32))
        return (hard_total, (loss_part, query_embedding_gradient, in_grad))
    initial = jnp.zeros((PAIRS, LATENT_DIM), jnp.float32)
    hard_total, outputs = lax.scan(per_group, initial, jnp.arange(group_count, dtype=jnp.int32))
    loss_parts, query_grads, in_grads = outputs
    query_embedding_gradient = query_grads.reshape(PAIRS, LATENT_DIM)
    passage_grad = in_grads.reshape(PAIRS, LATENT_DIM) + hard_total
    return (query_embedding_gradient, passage_grad, jnp.sum(loss_parts) / PAIRS)
```

```python
import functools
import math

import jax
import jax.numpy as jnp
from jax import lax
from jax.experimental import pallas as pl
from jax.experimental.pallas import tpu as pltpu
from jax.sharding import PartitionSpec as P

CAP = 10
PARTS = 4
F32, BF16 = jnp.float32, jnp.bfloat16
VMEM_BYTES = 58 * 1024 * 1024
PAIR = [(i, i ^ 2) for i in range(4)]
CORE = [(i, i ^ 1) for i in range(4)]
DIAG = [(i, i ^ 3) for i in range(4)]


def neighbour_groups():
    groups = []
    for a in range(2):
        for core in range(2):
            groups.append([m * 4 + (a ^ ((m // 4) % 2)) * 2 + core for m in range(32)])
    return groups


def dot(a, b):
    return jnp.dot(a, b, preferred_element_type=F32)


def dot_t(a, b):
    return lax.dot_general(a, b, (((1,), (1,)), ((), ())), preferred_element_type=F32)


def iota(shape, dim):
    return lax.broadcasted_iota(jnp.int32, shape, dim)


def params(**kw):
    return pltpu.CompilerParams(vmem_limit_bytes=VMEM_BYTES, **kw)


def whole(shape):
    return pl.BlockSpec(shape, lambda *_: (0,) * len(shape))


def serve_kernel(half_ref, code_ref, src_ref, *refs):
    out_ref = refs[-1]
    rows, width = src_ref.shape
    part = width // PARTS
    lane = iota((code_ref.shape[0], rows), 1)
    code = code_ref[...]
    acc = jnp.zeros(out_ref.shape, F32)
    for k in range(PARTS):
        hit = jnp.where(code == lane + rows * k, 1.0, 0.0).astype(BF16)
        acc += dot(hit, src_ref[:, k * part : (k + 1) * part])
    out_ref[...] = acc.astype(BF16)


def serve(half, codes, src, before=None):
    rows, width = src.shape
    n = codes.shape[0]
    tile = n // 8
    part = width // PARTS

    def at(i, half_ref):
        return (2 * i + half_ref[0], 0)

    extra = [] if before is None else [before]
    return pl.pallas_call(
        serve_kernel,
        grid_spec=pltpu.PrefetchScalarGridSpec(
            num_scalar_prefetch=1,
            grid=(4,),
            in_specs=[pl.BlockSpec((tile, 1), at), whole((rows, width))]
            + [pl.BlockSpec(memory_space=pl.ANY)] * len(extra),
            out_specs=pl.BlockSpec((tile, part), at),
        ),
        out_shape=jax.ShapeDtypeStruct((n, part), BF16),
        input_output_aliases={3: 0} if extra else {},
        compiler_params=params(),
        cost_estimate=pl.CostEstimate(
            flops=n * rows * width, bytes_accessed=4 * rows * width, transcendentals=0
        ),
        name="serve",
    )(half, codes, src, *extra)


def pack_kernel(place_ref, q_ref, out_ref):
    rows, width = q_ref.shape
    tile, part = out_ref.shape
    row = pl.program_id(0) * tile + iota((tile, rows), 0)
    acc = jnp.zeros((tile, part), F32)
    for k in range(PARTS):
        hit = jnp.where(row == place_ref[...] + CAP * k, 1.0, 0.0).astype(BF16)
        acc += dot(hit, q_ref[:, k * part : (k + 1) * part])
    out_ref[...] = acc.astype(BF16)


def pack(place_row, q, n):
    rows, width = q.shape
    tile = n // 8
    part = width // PARTS
    return pl.pallas_call(
        pack_kernel,
        grid=(8,),
        in_specs=[whole((1, rows)), whole((rows, width))],
        out_specs=pl.BlockSpec((tile, part), lambda i: (i, 0)),
        out_shape=jax.ShapeDtypeStruct((n, part), BF16),
        compiler_params=params(),
        cost_estimate=pl.CostEstimate(
            flops=2 * n * rows * width, bytes_accessed=4 * rows * width, transcendentals=0
        ),
        name="pack",
    )(place_row, q)


def scores_kernel(scale, q_ref, p0, p1, p2, p3, s_ref, stat_ref):
    rows = q_ref.shape[0]
    blocks = [dot_t(q_ref[...], p[...]) * scale for p in (p0, p1, p2, p3)]
    top = jnp.max(blocks[0], axis=1, keepdims=True)
    for b in blocks[1:]:
        top = jnp.maximum(top, jnp.max(b, axis=1, keepdims=True))
    total = jnp.zeros_like(top)
    for j, b in enumerate(blocks):
        total += jnp.sum(jnp.exp(b - top), axis=1, keepdims=True)
        s_ref[:, j * rows : (j + 1) * rows] = b
    eye = iota((rows, rows), 0) == iota((rows, rows), 1)
    diag = jnp.sum(jnp.where(eye, blocks[0], 0.0), axis=1, keepdims=True)
    lane = iota(stat_ref.shape, 1)
    stat_ref[...] = jnp.where(lane == 0, top, jnp.where(lane == 1, total, diag))


def scores(scale, q, passages):
    rows, width = q.shape
    full = whole((rows, width))
    return pl.pallas_call(
        functools.partial(scores_kernel, scale),
        grid=(1,),
        in_specs=[full] * 5,
        out_specs=[whole((rows, 4 * rows)), whole((rows, 128))],
        out_shape=[
            jax.ShapeDtypeStruct((rows, 4 * rows), F32),
            jax.ShapeDtypeStruct((rows, 128), F32),
        ],
        compiler_params=params(),
        cost_estimate=pl.CostEstimate(
            flops=8 * rows * rows * width,
            bytes_accessed=10 * rows * width,
            transcendentals=4 * rows * rows,
        ),
        name="scores",
    )(q, *passages)


def unpack_kernel(got_ref, place_ref, q_ref, f_ref, hard_ref):
    k = pl.program_id(0)
    rows = q_ref.shape[0]

    @pl.when(k == 0)
    def _():
        hard_ref[...] = jnp.zeros_like(hard_ref)

    lane = iota((rows, got_ref.shape[0]), 1)
    hit = jnp.where(lane == place_ref[...] + CAP * k, 1.0, 0.0).astype(BF16)
    fetched = dot(hit, got_ref[...])
    f_ref[...] = fetched.astype(BF16)
    hard_ref[...] += jnp.sum(fetched * q_ref[...].astype(F32), axis=1, keepdims=True)


def unpack(got, place_col, q):
    rows = q.shape[0]
    n, part = got.shape
    col = pl.BlockSpec((rows, part), lambda k: (0, k))
    return pl.pallas_call(
        unpack_kernel,
        grid=(PARTS,),
        in_specs=[whole((n, part)), whole((rows, 1)), col],
        out_specs=[col, whole((rows, 1))],
        out_shape=[
            jax.ShapeDtypeStruct((rows, part * PARTS), BF16),
            jax.ShapeDtypeStruct((rows, 1), F32),
        ],
        compiler_params=params(),
        cost_estimate=pl.CostEstimate(
            flops=2 * n * rows * part * PARTS,
            bytes_accessed=6 * rows * part * PARTS,
            transcendentals=0,
        ),
        name="unpack",
    )(got, place_col, q)


def weigh_kernel(
    scale, got_ref, place_ref, prow_ref, q_ref, first_ref, stat_ref, packed_ref,
    f_ref, sent_ref, wcol_ref, norm_ref, vec_ref, hard, lossv,
):
    i = pl.program_id(0)
    rows = q_ref.shape[0]

    @pl.when(i == 0)
    def _():
        hard[...] = first_ref[...]

    @pl.when(i < PARTS)
    def _():
        lane = iota((rows, got_ref.shape[0]), 1)
        hit = jnp.where(lane == place_ref[...] + CAP * i, 1.0, 0.0).astype(BF16)
        fetched = dot(hit, got_ref[...])
        f_ref[...] = fetched.astype(BF16)
        hard[...] += jnp.sum(fetched * q_ref[...].astype(F32), axis=1, keepdims=True)

    @pl.when(i == PARTS - 1)
    def _():
        score = hard[...] * scale
        top_in, total_in, diag = stat_ref[:, 0:1], stat_ref[:, 1:2], stat_ref[:, 2:3]
        top = jnp.maximum(top_in, score)
        norm = top + jnp.log(total_in * jnp.exp(top_in - top) + jnp.exp(score - top))
        weight = jnp.exp(score - norm).astype(BF16).astype(F32)
        wcol_ref[...] = weight
        norm_ref[...] = norm
        eye = iota((rows, rows), 0) == iota((rows, rows), 1)
        vec_ref[0:1, :] = jnp.sum(jnp.where(eye, norm, 0.0), axis=0, keepdims=True)
        vec_ref[1:2, :] = jnp.sum(jnp.where(eye, weight, 0.0), axis=0, keepdims=True)
        vec_ref[2:8, :] = jnp.zeros((6, rows), F32)
        loss = jnp.sum(norm - diag, axis=0, keepdims=True)
        high = loss.astype(BF16).astype(F32)
        mid = (loss - high).astype(BF16).astype(F32)
        low = loss - high - mid
        at = iota((1, 128), 1)
        lossv[...] = jnp.where(
            at == 0, high, jnp.where(at == 1, mid, jnp.where(at == 2, low, 0.0))
        )

    @pl.when(i >= PARTS)
    def _():
        tile, part = packed_ref.shape
        row = (i - PARTS) * tile + iota((tile, rows), 0)
        slot = row - CAP * lax.rem(lax.div(row, CAP), PARTS)
        weight = jnp.sum(
            jnp.where(slot == prow_ref[...], vec_ref[1:2, :], 0.0), axis=1, keepdims=True
        )
        sent_ref[:, :part] = (packed_ref[...].astype(F32) * weight).astype(BF16)
        row = (i - PARTS) * tile + iota((tile, 128), 0)
        first = lax.rem(row, CAP * PARTS) == 0
        sent_ref[:, part:] = jnp.where(first, lossv[...], 0.0).astype(BF16)


def weigh(scale, got, place_col, place_row, q, first, stats, packed):
    rows, width = q.shape
    n, part = got.shape
    tiles = 4
    tile = n // tiles
    lanes = packed.shape[1]
    col = pl.BlockSpec((rows, part), lambda i: (0, PARTS + jnp.minimum(i, PARTS - 1)))
    out_col = pl.BlockSpec((rows, part), lambda i: (0, jnp.minimum(i, PARTS - 1)))

    def row_at(i):
        return (jnp.maximum(i - PARTS, 0), 0)

    return pl.pallas_call(
        functools.partial(weigh_kernel, scale),
        grid=(PARTS + tiles,),
        in_specs=[
            whole((n, part)),
            whole((rows, 1)),
            whole((1, rows)),
            col,
            whole((rows, 1)),
            whole((rows, 128)),
            pl.BlockSpec((tile, lanes), row_at),
        ],
        out_specs=[
            out_col,
            pl.BlockSpec((tile, lanes + 128), row_at),
            whole((rows, 1)),
            whole((rows, 1)),
            whole((8, rows)),
        ],
        out_shape=[
            jax.ShapeDtypeStruct((rows, part * PARTS), BF16),
            jax.ShapeDtypeStruct((n, lanes + 128), BF16),
            jax.ShapeDtypeStruct((rows, 1), F32),
            jax.ShapeDtypeStruct((rows, 1), F32),
            jax.ShapeDtypeStruct((8, rows), F32),
        ],
        scratch_shapes=[pltpu.VMEM((rows, 1), F32), pltpu.VMEM((1, 128), F32)],
        compiler_params=params(),
        cost_estimate=pl.CostEstimate(
            flops=2 * n * rows * part * PARTS,
            bytes_accessed=8 * rows * width,
            transcendentals=4 * rows,
        ),
        name="weigh",
    )(got, place_col, place_row, q, first, stats, packed)


def qgrad_kernel(s_ref, norm_ref, wcol_ref, p0, p1, p2, p3, f0, f1, out_ref, w):
    t = pl.program_id(0)
    rows = out_ref.shape[0]

    @pl.when(t == 0)
    def _():
        for j in range(4):
            v = jnp.exp(s_ref[:, j * rows : (j + 1) * rows] - norm_ref[...])
            if j == 0:
                eye = iota((rows, rows), 0) == iota((rows, rows), 1)
                v = jnp.where(eye, v - 1.0, v)
            w[:, j * rows : (j + 1) * rows] = v.astype(BF16)

    fetched = jnp.where(t < PARTS, f0[...].astype(F32), f1[...].astype(F32))
    acc = wcol_ref[...] * fetched
    for j, p in enumerate((p0, p1, p2, p3)):
        acc += dot(w[:, j * rows : (j + 1) * rows], p[...])
    out_ref[...] = acc


def qgrad(s, norm, wcol, passages, fetched):
    rows, width = passages[0].shape
    tile = width // (2 * PARTS)
    col = pl.BlockSpec((rows, tile), lambda t: (0, t))
    low = pl.BlockSpec((rows, tile), lambda t: (0, jnp.minimum(t, PARTS - 1)))
    high = pl.BlockSpec((rows, tile), lambda t: (0, jnp.maximum(t - PARTS, 0)))
    return pl.pallas_call(
        qgrad_kernel,
        grid=(2 * PARTS,),
        in_specs=[whole(s.shape), whole((rows, 1)), whole((rows, 1))] + [col] * 4 + [low, high],
        out_specs=col,
        out_shape=jax.ShapeDtypeStruct((rows, width), F32),
        scratch_shapes=[pltpu.VMEM((rows, 4 * rows), BF16)],
        compiler_params=params(),
        cost_estimate=pl.CostEstimate(
            flops=8 * rows * rows * width,
            bytes_accessed=14 * rows * width,
            transcendentals=4 * rows * rows,
        ),
        name="qgrad",
    )(s, norm, wcol, *passages, *fetched)


def pgrad_kernel(scale, p_ref, q0, q1, q2, q3, n0, n1, n2, n3, out_ref, wt):
    t = pl.program_id(0)
    rows = p_ref.shape[0]
    tile = out_ref.shape[1]
    queries = (q0, q1, q2, q3)

    @pl.when(t == 0)
    def _():
        for j, (q, norm) in enumerate(zip(queries, (n0, n1, n2, n3))):
            w = jnp.exp(dot_t(p_ref[...], q[...]) * scale - norm[0:1, :])
            if j == 0:
                eye = iota((rows, rows), 0) == iota((rows, rows), 1)
                w = jnp.where(eye, w - 1.0, w)
            wt[:, j * rows : (j + 1) * rows] = w.astype(BF16)

    at = pl.ds(pl.multiple_of(t * tile, tile), tile)
    acc = jnp.zeros(out_ref.shape, F32)
    for j, q in enumerate(queries):
        acc += dot(wt[:, j * rows : (j + 1) * rows], q[:, at])
    out_ref[...] = acc


def pgrad(scale, p, queries, norms):
    rows, width = p.shape
    tile = width // 8
    full = whole((rows, width))
    return pl.pallas_call(
        functools.partial(pgrad_kernel, scale),
        grid=(8,),
        in_specs=[full] * 5 + [whole((8, rows))] * 4,
        out_specs=pl.BlockSpec((rows, tile), lambda t: (0, t)),
        out_shape=jax.ShapeDtypeStruct((rows, width), F32),
        scratch_shapes=[pltpu.VMEM((rows, 4 * rows), BF16)],
        compiler_params=params(),
        cost_estimate=pl.CostEstimate(
            flops=16 * rows * rows * width,
            bytes_accessed=14 * rows * width,
            transcendentals=4 * rows * rows,
        ),
        name="pgrad",
    )(p, *queries, *norms)


def loss_kernel(got_ref, out_ref):
    both = jnp.sum(got_ref[...].astype(F32), axis=0, keepdims=True)
    out_ref[...] = jnp.broadcast_to(jnp.sum(both, axis=1, keepdims=True), out_ref.shape)


def losses(got, part):
    n = got.shape[0]
    return pl.pallas_call(
        loss_kernel,
        grid=(1,),
        in_specs=[pl.BlockSpec((n, 128), lambda i: (0, part // 128))],
        out_specs=whole((8, 128)),
        out_shape=jax.ShapeDtypeStruct((8, 128), F32),
        compiler_params=params(),
        name="losses",
    )(got)


def finish_kernel(code_ref, got_ref, part_ref, out_ref):
    k = pl.program_id(0)
    rows, part = out_ref.shape
    hit = jnp.where(
        code_ref[...] == iota((rows, code_ref.shape[1]), 0) + rows * k, 1.0, 0.0
    ).astype(BF16)
    out_ref[...] = part_ref[...] + dot(hit, got_ref[...])


def finish(codes_row, got, partial_grad):
    rows, width = partial_grad.shape
    part = width // PARTS
    col = pl.BlockSpec((rows, part), lambda k: (0, k))
    return pl.pallas_call(
        finish_kernel,
        grid=(PARTS,),
        in_specs=[whole(codes_row.shape), whole((got.shape[0], part)), col],
        out_specs=col,
        out_shape=jax.ShapeDtypeStruct((rows, width), F32),
        compiler_params=params(),
        cost_estimate=pl.CostEstimate(
            flops=2 * got.shape[0] * rows * width, bytes_accessed=9 * rows * width, transcendentals=0
        ),
        name="finish",
    )(codes_row, got, partial_grad)


def shards(queries, passages, hard_owner, hard_row):
    rows, width = queries.shape
    n_dp = lax.axis_size("dp")
    n_blk = lax.axis_size("blk")
    scale = 2.0 / math.sqrt(width)
    half = lax.rem(lax.axis_index("dp") // 4, 2).astype(jnp.int32)
    chunk = CAP * PARTS
    n = n_dp * chunk

    def permute(x, table):
        return lax.ppermute(x, "blk", table)

    def exchange(x, groups):
        return lax.all_to_all(x, ("dp", "blk"), 0, 0, axis_index_groups=groups, tiled=True)

    p_halves = [passages[:, : width // 2], passages[:, width // 2 :]]
    pair_halves = [permute(p, PAIR) for p in p_halves]
    p_core = permute(passages, CORE)

    owner = hard_owner[:, 0]
    row = hard_row[:, 0]
    hits = (owner[:, None] == jnp.arange(n_dp, dtype=jnp.int32)[None, :]).astype(BF16)
    order = jnp.arange(rows, dtype=jnp.int32)
    before = (order[:, None] > order[None, :]).astype(BF16)
    slot = jnp.sum(dot(before, hits) * hits.astype(F32), axis=1).astype(jnp.int32)
    place = owner * chunk + slot
    place_col, place_row = place.reshape(rows, 1), place.reshape(1, rows)
    at = jnp.arange(n, dtype=jnp.int32)
    part_of = (at // CAP) % PARTS
    match = (at - CAP * part_of)[:, None] == place[None, :]
    codes = jnp.sum(jnp.where(match, row[None, :] + 1, 0), axis=1)
    codes = jnp.where(codes > 0, codes - 1 + rows * part_of, -1)
    groups = neighbour_groups()
    asked = exchange(codes.reshape(n_dp, chunk), groups).reshape(n)
    asked_col = asked.reshape(n, 1)
    asked_pair = permute(asked, PAIR)

    here, there = half.reshape(1), (1 - half).reshape(1)
    own_part = [serve(here, asked_col, p) for p in p_halves]
    got = [
        exchange(serve(there, asked_col, p, o), groups) for p, o in zip(pair_halves, own_part)
    ]

    q_late, _ = lax.optimization_barrier((queries, asked_pair))
    q_pair = permute(q_late, PAIR)
    q_core = permute(queries, CORE)
    q_diag = permute(q_pair, CORE)

    p_pair = jnp.concatenate(pair_halves, axis=1)
    p_diag = permute(p_pair, CORE)
    passage_blocks = (passages, p_core, p_pair, p_diag)
    packed = pack(place_row, queries, n)
    s, stats = scores(scale, queries, passage_blocks)
    fetched0, first = unpack(got[0], place_col, queries)
    fetched1, sent, wcol, norm, vectors = weigh(
        scale, got[1], place_col, place_row, queries, first, stats, packed
    )
    terms = lax.all_to_all(sent, "dp", 0, 0, tiled=True)

    norms = (vectors, permute(vectors, CORE), permute(vectors, PAIR), permute(vectors, DIAG))
    query_gradient = qgrad(s, norm, wcol, passage_blocks, (fetched0, fetched1))
    partial_grad = pgrad(scale, passages, (queries, q_core, q_pair, q_diag), norms)

    loss_dp = losses(terms, width // PARTS)
    loss_all = loss_dp + permute(loss_dp, CORE) + permute(loss_dp, PAIR) + permute(loss_dp, DIAG)
    loss = loss_all[0, 0] / (rows * n_blk * n_dp)

    source_half = (at // chunk // 4) % 2
    owned = jnp.where(source_half == half, asked, asked_pair)
    passage_gradient = finish(owned.reshape(1, n), terms, partial_grad)
    return query_gradient, passage_gradient, loss


def solution(mesh):
    spec = P(("dp", "blk"), None)
    return jax.shard_map(
        shards,
        mesh=mesh,
        in_specs=(spec,) * 4,
        out_specs=(spec, spec, P()),
        check_vma=False,
    )
```

```python
import functools
import math

import jax
import jax.numpy as jnp
from jax import lax
from jax.experimental import pallas as pl
from jax.experimental.pallas import tpu as pltpu
from jax.sharding import PartitionSpec as P

MAIN, EXTRA = 8, 2
PARTS = 4
F32, BF16 = jnp.float32, jnp.bfloat16
VMEM_BYTES = 58 * 1024 * 1024
SMALL_BYTES = 32 * 1024 * 1024
PAIR = [(i, i ^ 2) for i in range(4)]
CORE = [(i, i ^ 1) for i in range(4)]
DIAG = [(i, i ^ 3) for i in range(4)]


def position(dp):
    return dp // 4 % 2 * 16 + dp // 8 * 4 + dp % 4


def order(core):
    return sorted(range(32), key=position, reverse=bool(core))


NEIGHBOURS = [
    [m * 4 + (a ^ (m // 4 % 2)) * 2 + core for m in order(core)] for a in range(2) for core in range(2)
]
COLUMNS = [[m * 4 + a * 2 + core for m in order(core)] for a in range(2) for core in range(2)]


def dot(a, b):
    return jnp.dot(a, b, preferred_element_type=F32)


def dot_t(a, b):
    return lax.dot_general(a, b, (((1,), (1,)), ((), ())), preferred_element_type=F32)


def iota(shape, dim):
    return lax.broadcasted_iota(jnp.int32, shape, dim)


def params(limit=VMEM_BYTES):
    return pltpu.CompilerParams(vmem_limit_bytes=limit)


def whole(shape):
    return pl.BlockSpec(shape, lambda *_: (0,) * len(shape))


def one(hit):
    return jnp.where(hit, 1.0, 0.0).astype(BF16)


def chunk_row(shape, dim):
    r = iota(shape, dim)
    return r, r - EXTRA * lax.div(lax.rem(r, MAIN), EXTRA)


def serve_kernel(half_ref, code_ref, own_ref, pair_ref, out_ref):
    rows, width = own_ref.shape
    part = width // PARTS
    half_rows = code_ref.shape[0] // 2
    lane = iota((half_rows, rows), 1)
    half = half_ref[0]
    for src, which in ((own_ref, half), (pair_ref, 1 - half)):
        at = pl.ds(pl.multiple_of(which * half_rows, half_rows), half_rows)
        code = code_ref[at, :]
        main = one(code[:, 0:1] == lane)
        acc = jnp.zeros((half_rows, part), F32)
        for k in range(PARTS):
            values = src[:, k * part : (k + 1) * part]
            out_ref[at, k * part : (k + 1) * part] = dot(main, values).astype(BF16)
            acc += dot(one(code[:, 1:2] == lane + rows * k), values)
        out_ref[at, width:] = acc.astype(BF16)


def serve(half, codes, own, pair):
    rows, width = own.shape
    n = codes.shape[0]
    lanes = width + width // PARTS
    return pl.pallas_call(
        serve_kernel,
        grid=(1,),
        in_specs=[pl.BlockSpec(memory_space=pltpu.SMEM)]
        + [whole(codes.shape), whole(own.shape), whole(pair.shape)],
        out_specs=whole((n, lanes)),
        out_shape=jax.ShapeDtypeStruct((n, lanes), BF16),
        compiler_params=params(),
        cost_estimate=pl.CostEstimate(
            flops=4 * n * rows * width, bytes_accessed=7 * rows * width, transcendentals=0
        ),
        name="serve",
    )(half, codes, own, pair)


def pack_kernel(place_ref, q_ref, out_ref, acc):
    k = pl.program_id(0)
    rows = q_ref.shape[0]
    n = out_ref.shape[0]

    @pl.when(k == 0)
    def _():
        acc[...] = jnp.zeros_like(acc)

    @pl.when(k < PARTS)
    def _():
        row = iota((n, rows), 0)
        out_ref[...] = dot(one(row == place_ref[0:1, :]), q_ref[...]).astype(BF16)
        acc[...] += dot(one(row == place_ref[1:2, :] + EXTRA * k), q_ref[...])

    @pl.when(k == PARTS)
    def _():
        out_ref[...] = acc[...].astype(BF16)


def pack(place_rows, q, n):
    rows, width = q.shape
    part = width // PARTS
    return pl.pallas_call(
        pack_kernel,
        grid=(PARTS + 1,),
        in_specs=[
            whole((2, rows)),
            pl.BlockSpec((rows, part), lambda k: (0, jnp.minimum(k, PARTS - 1))),
        ],
        out_specs=pl.BlockSpec((n, part), lambda k: (0, k)),
        out_shape=jax.ShapeDtypeStruct((n, width + part + 128), BF16),
        scratch_shapes=[pltpu.VMEM((n, part), F32)],
        compiler_params=params(),
        cost_estimate=pl.CostEstimate(
            flops=4 * n * rows * width, bytes_accessed=5 * rows * width, transcendentals=0
        ),
        name="pack",
    )(place_rows, q)


def scores_kernel(scale, q_ref, p0, p1, p2, p3, s_ref, stat_ref):
    rows = q_ref.shape[0]
    blocks = [dot_t(q_ref[...], p[...]) * scale for p in (p0, p1, p2, p3)]
    top = jnp.max(blocks[0], axis=1, keepdims=True)
    for b in blocks[1:]:
        top = jnp.maximum(top, jnp.max(b, axis=1, keepdims=True))
    total = jnp.zeros_like(top)
    for j, b in enumerate(blocks):
        total += jnp.sum(jnp.exp(b - top), axis=1, keepdims=True)
        s_ref[:, j * rows : (j + 1) * rows] = b
    eye = iota((rows, rows), 0) == iota((rows, rows), 1)
    diag = jnp.sum(jnp.where(eye, blocks[0], 0.0), axis=1, keepdims=True)
    lane = iota(stat_ref.shape, 1)
    stat_ref[...] = jnp.where(lane == 0, top, jnp.where(lane == 1, total, diag))


def scores(scale, q, passages):
    rows, width = q.shape
    full = whole((rows, width))
    return pl.pallas_call(
        functools.partial(scores_kernel, scale),
        grid=(1,),
        in_specs=[full] * 5,
        out_specs=[whole((rows, 4 * rows)), whole((rows, 128))],
        out_shape=[
            jax.ShapeDtypeStruct((rows, 4 * rows), F32),
            jax.ShapeDtypeStruct((rows, 128), F32),
        ],
        compiler_params=params(),
        cost_estimate=pl.CostEstimate(
            flops=8 * rows * rows * width,
            bytes_accessed=10 * rows * width,
            transcendentals=4 * rows * rows,
        ),
        name="scores",
    )(q, *passages)


def take_rows(got_ref, place_ref, q_ref, f_ref):
    rows, width = q_ref.shape
    part = width // PARTS
    lane = iota((rows, got_ref.shape[0]), 1)
    main = one(lane == place_ref[:, 0:1])
    score = jnp.zeros((rows, 1), F32)
    for k in range(PARTS):
        at = slice(k * part, (k + 1) * part)
        fetched = dot(main, got_ref[:, at])
        fetched += dot(one(lane == place_ref[:, 1:2] + EXTRA * k), got_ref[:, width:])
        f_ref[:, at] = fetched.astype(BF16)
        score += jnp.sum(fetched * q_ref[:, at].astype(F32), axis=1, keepdims=True)
    return score


def unpack_kernel(got_ref, place_ref, q_ref, f_ref, hard_ref):
    hard_ref[...] = take_rows(got_ref, place_ref, q_ref, f_ref)


def unpack(got, place_cols, q):
    rows, width = q.shape[0], q.shape[1] // 2
    return pl.pallas_call(
        unpack_kernel,
        grid=(1,),
        in_specs=[whole(got.shape), whole((rows, 2)), pl.BlockSpec((rows, width), lambda i: (0, 0))],
        out_specs=[whole((rows, width)), whole((rows, 1))],
        out_shape=[
            jax.ShapeDtypeStruct((rows, width), BF16),
            jax.ShapeDtypeStruct((rows, 1), F32),
        ],
        compiler_params=params(),
        cost_estimate=pl.CostEstimate(
            flops=4 * got.shape[0] * rows * width,
            bytes_accessed=7 * rows * width,
            transcendentals=0,
        ),
        name="unpack",
    )(got, place_cols, q)


def soft_kernel(
    scale, got_ref, place_ref, q_ref, first_ref, stat_ref, f_ref, wcol_ref, norm_ref, vec_ref
):
    rows = q_ref.shape[0]
    score = (first_ref[...] + take_rows(got_ref, place_ref, q_ref, f_ref)) * scale
    top_in, total_in, diag = stat_ref[:, 0:1], stat_ref[:, 1:2], stat_ref[:, 2:3]
    top = jnp.maximum(top_in, score)
    norm = top + jnp.log(total_in * jnp.exp(top_in - top) + jnp.exp(score - top))
    weight = jnp.exp(score - norm).astype(BF16).astype(F32)
    wcol_ref[...] = weight
    norm_ref[...] = norm
    eye = iota((rows, rows), 0) == iota((rows, rows), 1)
    vec_ref[0:1, :] = jnp.sum(jnp.where(eye, norm, 0.0), axis=0, keepdims=True)
    vec_ref[1:2, :] = jnp.sum(jnp.where(eye, weight, 0.0), axis=0, keepdims=True)
    loss = jnp.sum(norm - diag, axis=0, keepdims=True)
    vec_ref[2:3, :] = jnp.broadcast_to(loss, (1, rows))
    vec_ref[3:8, :] = jnp.zeros((5, rows), F32)


def soft(scale, got, place_cols, q, first, stats):
    rows, width = q.shape[0], q.shape[1] // 2
    return pl.pallas_call(
        functools.partial(soft_kernel, scale),
        grid=(1,),
        in_specs=[
            whole(got.shape),
            whole((rows, 2)),
            pl.BlockSpec((rows, width), lambda i: (0, 1)),
            whole((rows, 1)),
            whole((rows, 128)),
        ],
        out_specs=[whole((rows, width)), whole((rows, 1)), whole((rows, 1)), whole((8, rows))],
        out_shape=[
            jax.ShapeDtypeStruct((rows, width), BF16),
            jax.ShapeDtypeStruct((rows, 1), F32),
            jax.ShapeDtypeStruct((rows, 1), F32),
            jax.ShapeDtypeStruct((8, rows), F32),
        ],
        compiler_params=params(),
        cost_estimate=pl.CostEstimate(
            flops=4 * got.shape[0] * rows * width,
            bytes_accessed=7 * rows * width,
            transcendentals=4 * rows,
        ),
        name="soft",
    )(got, place_cols, q, first, stats)


def stamp_kernel(place_ref, v0, v1, v2, v3, packed_ref, out_ref):
    n, rows = out_ref.shape[0], place_ref.shape[1]
    row, base = chunk_row((n, rows), 0)
    weight = v0[1:2, :]
    main = jnp.sum(jnp.where(row == place_ref[0:1, :], weight, 0.0), axis=1, keepdims=True)
    extra = jnp.sum(jnp.where(base == place_ref[1:2, :], weight, 0.0), axis=1, keepdims=True)
    loss = v0[2:3, 0:128] + v1[2:3, 0:128] + v2[2:3, 0:128] + v3[2:3, 0:128]
    high = loss.astype(BF16).astype(F32)
    mid = (loss - high).astype(BF16).astype(F32)
    low = loss - high - mid
    lane = iota((1, 128), 1)
    parts = jnp.where(lane == 2, high, jnp.where(lane == 3, mid, jnp.where(lane == 4, low, 0.0)))
    first = lax.rem(iota(out_ref.shape, 0), MAIN) == 0
    lane = iota(out_ref.shape, 1)
    notes = jnp.where(lane == 0, main, jnp.where(lane == 1, extra, jnp.where(first, parts, 0.0)))
    out_ref[...] = notes.astype(BF16)


def stamp(place_rows, vectors, packed):
    n, lanes = packed.shape
    return pl.pallas_call(
        stamp_kernel,
        grid=(1,),
        in_specs=[whole(place_rows.shape)]
        + [whole(v.shape) for v in vectors]
        + [pl.BlockSpec(memory_space=pl.ANY)],
        out_specs=pl.BlockSpec((n, 128), lambda i: (0, lanes // 128 - 1)),
        out_shape=jax.ShapeDtypeStruct((n, lanes), BF16),
        input_output_aliases={5: 0},
        compiler_params=params(60 * 1024 * 1024),
        name="stamp",
    )(place_rows, *vectors, packed)


def qgrad_kernel(s_ref, norm_ref, wcol_ref, p0, p1, p2, p3, f0, f1, out_ref, w):
    t = pl.program_id(0)
    rows = out_ref.shape[0]

    @pl.when(t == 0)
    def _():
        for j in range(4):
            v = jnp.exp(s_ref[:, j * rows : (j + 1) * rows] - norm_ref[...])
            if j == 0:
                eye = iota((rows, rows), 0) == iota((rows, rows), 1)
                v = jnp.where(eye, v - 1.0, v)
            w[:, j * rows : (j + 1) * rows] = v.astype(BF16)

    fetched = jnp.where(t < PARTS, f0[...].astype(F32), f1[...].astype(F32))
    acc = wcol_ref[...] * fetched
    for j, p in enumerate((p0, p1, p2, p3)):
        acc += dot(w[:, j * rows : (j + 1) * rows], p[...])
    out_ref[...] = acc


def qgrad(s, norm, wcol, passages, fetched):
    rows, width = passages[0].shape
    tile = width // (2 * PARTS)
    col = pl.BlockSpec((rows, tile), lambda t: (0, t))
    low = pl.BlockSpec((rows, tile), lambda t: (0, jnp.minimum(t, PARTS - 1)))
    high = pl.BlockSpec((rows, tile), lambda t: (0, jnp.maximum(t - PARTS, 0)))
    return pl.pallas_call(
        qgrad_kernel,
        grid=(2 * PARTS,),
        in_specs=[whole(s.shape), whole((rows, 1)), whole((rows, 1))] + [col] * 4 + [low, high],
        out_specs=col,
        out_shape=jax.ShapeDtypeStruct((rows, width), F32),
        scratch_shapes=[pltpu.VMEM((rows, 4 * rows), BF16)],
        compiler_params=params(),
        cost_estimate=pl.CostEstimate(
            flops=8 * rows * rows * width,
            bytes_accessed=14 * rows * width,
            transcendentals=4 * rows * rows,
        ),
        name="qgrad",
    )(s, norm, wcol, *passages, *fetched)


def pgrad_kernel(scale, p_ref, q0, q1, q2, q3, n0, n1, n2, n3, out_ref, wt):
    t = pl.program_id(0)
    rows = p_ref.shape[0]
    tile = out_ref.shape[1]
    queries = (q0, q1, q2, q3)

    @pl.when(t == 0)
    def _():
        for j, (q, norm) in enumerate(zip(queries, (n0, n1, n2, n3))):
            w = jnp.exp(dot_t(p_ref[...], q[...]) * scale - norm[0:1, :])
            if j == 0:
                eye = iota((rows, rows), 0) == iota((rows, rows), 1)
                w = jnp.where(eye, w - 1.0, w)
            wt[:, j * rows : (j + 1) * rows] = w.astype(BF16)

    at = pl.ds(pl.multiple_of(t * tile, tile), tile)
    acc = jnp.zeros(out_ref.shape, F32)
    for j, q in enumerate(queries):
        acc += dot(wt[:, j * rows : (j + 1) * rows], q[:, at])
    out_ref[...] = acc


def pgrad(scale, p, queries, norms):
    rows, width = p.shape
    tile = width // 8
    full = whole((rows, width))
    return pl.pallas_call(
        functools.partial(pgrad_kernel, scale),
        grid=(8,),
        in_specs=[full] * 5 + [whole((8, rows))] * 4,
        out_specs=pl.BlockSpec((rows, tile), lambda t: (0, t)),
        out_shape=jax.ShapeDtypeStruct((rows, width), F32),
        scratch_shapes=[pltpu.VMEM((rows, 4 * rows), BF16)],
        compiler_params=params(SMALL_BYTES),
        cost_estimate=pl.CostEstimate(
            flops=16 * rows * rows * width,
            bytes_accessed=14 * rows * width,
            transcendentals=4 * rows * rows,
        ),
        name="pgrad",
    )(p, *queries, *norms)


def finish_kernel(
    mean, half_ref, own_ref, pair_ref, main_ref, extra_ref, note_ref, part_ref, out_ref, mean_ref
):
    rows, width = out_ref.shape
    n, part = extra_ref.shape
    here = lax.div(iota((1, n), 1), n // 2) == half_ref[0]
    codes = jnp.where(here, own_ref[...], pair_ref[...])
    row = iota((rows, n), 0)
    hit = one(codes[0:1, :] == row)
    weight = note_ref[:, 0:1].astype(F32)
    late = (extra_ref[...].astype(F32) * note_ref[:, 1:2].astype(F32)).astype(BF16)
    for q in range(width // part):
        at = slice(q * part, (q + 1) * part)
        terms = (main_ref[:, at].astype(F32) * weight).astype(BF16)
        k = pl.program_id(0) * (width // part) + q
        acc = part_ref[:, at] + dot(hit, terms)
        out_ref[:, at] = acc + dot(one(codes[1:2, :] == row + rows * k), late)

    @pl.when(pl.program_id(0) == 0)
    def _():
        lane = iota(note_ref.shape, 1)
        parts = jnp.where((lane >= 2) & (lane <= 4), note_ref[...].astype(F32), 0.0)
        total = jnp.sum(parts, axis=0, keepdims=True)
        mean_ref[...] = jnp.sum(total, axis=1, keepdims=True) * mean


def finish(mean, half, own_rows, pair_rows, got, partial_grad):
    rows, width = partial_grad.shape
    n = got.shape[0]
    part = width // PARTS
    steps = 2
    col = pl.BlockSpec((rows, width // steps), lambda t: (0, t))
    return pl.pallas_call(
        functools.partial(finish_kernel, mean),
        grid=(steps,),
        in_specs=[
            pl.BlockSpec(memory_space=pltpu.SMEM),
            whole((2, n)),
            whole((2, n)),
            pl.BlockSpec((n, width // steps), lambda t: (0, t)),
            pl.BlockSpec((n, part), lambda t: (0, PARTS)),
            pl.BlockSpec((n, 128), lambda t: (0, (PARTS + 1) * part // 128)),
            col,
        ],
        out_specs=[col, whole((1, 1))],
        out_shape=[
            jax.ShapeDtypeStruct((rows, width), F32),
            jax.ShapeDtypeStruct((1, 1), F32),
        ],
        compiler_params=params(),
        cost_estimate=pl.CostEstimate(
            flops=4 * n * rows * width, bytes_accessed=11 * rows * width, transcendentals=0
        ),
        name="finish",
    )(half, own_rows, pair_rows, got, got, got, partial_grad)


def shards(queries, passages, hard_owner, hard_row):
    rows, width = queries.shape
    n_dp = lax.axis_size("dp")
    n_blk = lax.axis_size("blk")
    scale = 2.0 / math.sqrt(width)
    core = lax.rem(lax.axis_index("blk"), 2).astype(jnp.int32)
    half = lax.rem(lax.axis_index("dp") // 4, 2).astype(jnp.int32)
    half = lax.rem(half + core, 2).reshape(1)
    n = n_dp * MAIN

    def permute(x, table):
        return lax.ppermute(x, "blk", table)

    def exchange(x, groups):
        return lax.all_to_all(x, ("dp", "blk"), 0, 0, axis_index_groups=groups, tiled=True)

    p_low = passages[:, : width // 2]
    later, _ = lax.optimization_barrier((passages, p_low))
    p_halves = [p_low, later[:, width // 2 :]]
    pair_halves = [permute(p, PAIR) for p in p_halves]
    p_core = permute(passages, CORE)

    owner = hard_owner[:, 0]
    row = hard_row[:, 0]
    hits = (owner[:, None] == jnp.arange(n_dp, dtype=jnp.int32)[None, :]).astype(BF16)
    index = jnp.arange(rows, dtype=jnp.int32)
    before = (index[:, None] > index[None, :]).astype(BF16)
    slot = jnp.sum(dot(before, hits) * hits.astype(F32), axis=1).astype(jnp.int32)
    place = position(owner)
    chunk = jnp.where(core == 1, n_dp - 1 - place, place) * MAIN
    place_main = jnp.where(slot < MAIN, chunk + slot, -1)
    place_extra = jnp.where(slot < MAIN, -2 * MAIN, chunk + slot - MAIN)
    place_rows = jnp.stack([place_main, place_extra], axis=0)
    place_cols = jnp.stack([place_main, place_extra], axis=1)
    at = jnp.arange(n, dtype=jnp.int32)
    quarter = at % MAIN // EXTRA
    match = at[:, None] == place_main[None, :]
    code_main = jnp.sum(jnp.where(match, row[None, :] + 1, 0), axis=1) - 1
    match = (at - EXTRA * quarter)[:, None] == place_extra[None, :]
    code_extra = jnp.sum(jnp.where(match, row[None, :] + 1, 0), axis=1)
    code_extra = jnp.where(code_extra > 0, code_extra - 1 + rows * quarter, -1)
    codes = jnp.concatenate([code_main.reshape(n_dp, MAIN), code_extra.reshape(n_dp, MAIN)], axis=1)
    packed = pack(place_rows, queries, n)
    asked, packed = lax.optimization_barrier((exchange(codes, NEIGHBOURS), packed))
    asked = asked.reshape(n_dp, 2, MAIN)
    asked_cols = asked.transpose(0, 2, 1).reshape(n, 2)
    asked_rows = asked.transpose(1, 0, 2).reshape(2, n)
    asked_pair = permute(asked_rows, PAIR)

    got = [
        exchange(serve(half, asked_cols, p, o), NEIGHBOURS) for p, o in zip(p_halves, pair_halves)
    ]

    cut = 3 * rows // 4
    q_first, _ = lax.optimization_barrier((queries[:cut], codes))
    q_pair_first = permute(q_first, PAIR)
    q_core = permute(queries, CORE)

    p_pair = jnp.concatenate(pair_halves, axis=1)
    p_diag = permute(p_pair, CORE)
    passage_blocks = (passages, p_core, p_pair, p_diag)
    s, stats = scores(scale, queries, passage_blocks)
    fetched0, first = unpack(got[0], place_cols, queries)
    fetched1, wcol, norm, vectors = soft(scale, got[1], place_cols, queries, first, stats)

    vectors = (vectors, permute(vectors, CORE), permute(vectors, PAIR), permute(vectors, DIAG))

    q_last, *_ = lax.optimization_barrier((queries[cut:], *vectors[1:]))
    q_pair_last = permute(q_last, PAIR)
    sent = stamp(place_rows, vectors, packed)
    q_pair_first, sent = lax.optimization_barrier((q_pair_first, sent))
    q_pair = jnp.concatenate([q_pair_first, q_pair_last], axis=0)
    q_diag = permute(q_pair, CORE)
    terms = exchange(sent, COLUMNS)

    query_gradient = qgrad(s, norm, wcol, passage_blocks, (fetched0, fetched1))
    partial_grad = pgrad(scale, passages, (queries, q_core, q_pair, q_diag), vectors)
    mean = 1.0 / (rows * n_blk * n_dp)
    passage_gradient, loss = finish(mean, half, asked_rows, asked_pair, terms, partial_grad)
    return query_gradient, passage_gradient, loss.reshape(())


def solution(mesh):
    spec = P(("dp", "blk"), None)
    return jax.shard_map(
        shards,
        mesh=mesh,
        in_specs=(spec,) * 4,
        out_specs=(spec, spec, P()),
        check_vma=False,
    )
```

```python
import functools
import math

import jax
import jax.numpy as jnp
from jax import lax
from jax.experimental import pallas as pl
from jax.experimental.pallas import tpu as pltpu
from jax.sharding import PartitionSpec as P

MAIN, EXTRA = 8, 2
PARTS = 4
F32, BF16 = jnp.float32, jnp.bfloat16
VMEM_BYTES = 58 * 1024 * 1024
SMALL_BYTES = 32 * 1024 * 1024
PAIR = [(i, i ^ 2) for i in range(4)]
CORE = [(i, i ^ 1) for i in range(4)]
DIAG = [(i, i ^ 3) for i in range(4)]


def position(dp):
    return dp // 4 % 2 * 16 + dp // 8 * 4 + dp % 4


def order(core):
    return sorted(range(32), key=position, reverse=bool(core))


NEIGHBOURS = [
    [m * 4 + (a ^ (m // 4 % 2)) * 2 + core for m in order(core)] for a in range(2) for core in range(2)
]
COLUMNS = [[m * 4 + a * 2 + core for m in order(core)] for a in range(2) for core in range(2)]


def dot(a, b):
    return jnp.dot(a, b, preferred_element_type=F32)


def dot_t(a, b):
    return lax.dot_general(a, b, (((1,), (1,)), ((), ())), preferred_element_type=F32)


def iota(shape, dim):
    return lax.broadcasted_iota(jnp.int32, shape, dim)


def params(limit=VMEM_BYTES):
    return pltpu.CompilerParams(vmem_limit_bytes=limit)


def whole(shape):
    return pl.BlockSpec(shape, lambda *_: (0,) * len(shape))


def one(hit):
    return jnp.where(hit, 1.0, 0.0).astype(BF16)


def chunk_row(shape, dim):
    r = iota(shape, dim)
    return r, r - EXTRA * lax.div(lax.rem(r, MAIN), EXTRA)


def serve_kernel(half_ref, code_ref, own_ref, pair_ref, out_ref):
    rows, width = own_ref.shape
    part = width // PARTS
    half_rows = code_ref.shape[0] // 2
    lane = iota((half_rows, rows), 1)
    half = half_ref[0]
    for src, which in ((own_ref, half), (pair_ref, 1 - half)):
        at = pl.ds(pl.multiple_of(which * half_rows, half_rows), half_rows)
        code = code_ref[at, :]
        main = one(code[:, 0:1] == lane)
        acc = jnp.zeros((half_rows, part), F32)
        for k in range(PARTS):
            values = src[:, k * part : (k + 1) * part]
            out_ref[at, k * part : (k + 1) * part] = dot(main, values).astype(BF16)
            acc += dot(one(code[:, 1:2] == lane + rows * k), values)
        out_ref[at, width:] = acc.astype(BF16)


def serve(half, codes, own, pair):
    rows, width = own.shape
    n = codes.shape[0]
    lanes = width + width // PARTS
    return pl.pallas_call(
        serve_kernel,
        grid=(1,),
        in_specs=[pl.BlockSpec(memory_space=pltpu.SMEM)]
        + [whole(codes.shape), whole(own.shape), whole(pair.shape)],
        out_specs=whole((n, lanes)),
        out_shape=jax.ShapeDtypeStruct((n, lanes), BF16),
        compiler_params=params(SMALL_BYTES),
        cost_estimate=pl.CostEstimate(
            flops=4 * n * rows * width, bytes_accessed=7 * rows * width, transcendentals=0
        ),
        name="serve",
    )(half, codes, own, pair)


def pack_kernel(place_ref, q_ref, out_ref, acc):
    k = pl.program_id(0)
    rows = q_ref.shape[0]
    n = out_ref.shape[0]

    @pl.when(k == 0)
    def _():
        acc[...] = jnp.zeros_like(acc)

    @pl.when(k < PARTS)
    def _():
        row = iota((n, rows), 0)
        out_ref[...] = dot(one(row == place_ref[0:1, :]), q_ref[...]).astype(BF16)
        acc[...] += dot(one(row == place_ref[1:2, :] + EXTRA * k), q_ref[...])

    @pl.when(k == PARTS)
    def _():
        out_ref[...] = acc[...].astype(BF16)


def pack(place_rows, q, n):
    rows, width = q.shape
    part = width // PARTS
    return pl.pallas_call(
        pack_kernel,
        grid=(PARTS + 1,),
        in_specs=[
            whole((2, rows)),
            pl.BlockSpec((rows, part), lambda k: (0, jnp.minimum(k, PARTS - 1))),
        ],
        out_specs=pl.BlockSpec((n, part), lambda k: (0, k)),
        out_shape=jax.ShapeDtypeStruct((n, width + part + 128), BF16),
        scratch_shapes=[pltpu.VMEM((n, part), F32)],
        compiler_params=params(),
        cost_estimate=pl.CostEstimate(
            flops=4 * n * rows * width, bytes_accessed=5 * rows * width, transcendentals=0
        ),
        name="pack",
    )(place_rows, q)


def scores_kernel(scale, q_ref, p0, p1, p2, p3, s_ref, stat_ref):
    rows = q_ref.shape[0]
    blocks = [dot_t(q_ref[...], p[...]) * scale for p in (p0, p1, p2, p3)]
    top = jnp.max(blocks[0], axis=1, keepdims=True)
    for b in blocks[1:]:
        top = jnp.maximum(top, jnp.max(b, axis=1, keepdims=True))
    total = jnp.zeros_like(top)
    for j, b in enumerate(blocks):
        total += jnp.sum(jnp.exp(b - top), axis=1, keepdims=True)
        s_ref[:, j * rows : (j + 1) * rows] = b
    eye = iota((rows, rows), 0) == iota((rows, rows), 1)
    diag = jnp.sum(jnp.where(eye, blocks[0], 0.0), axis=1, keepdims=True)
    lane = iota(stat_ref.shape, 1)
    stat_ref[...] = jnp.where(lane == 0, top, jnp.where(lane == 1, total, diag))


def scores(scale, q, passages):
    rows, width = q.shape
    full = whole((rows, width))
    return pl.pallas_call(
        functools.partial(scores_kernel, scale),
        grid=(1,),
        in_specs=[full] * 5,
        out_specs=[whole((rows, 4 * rows)), whole((rows, 128))],
        out_shape=[
            jax.ShapeDtypeStruct((rows, 4 * rows), F32),
            jax.ShapeDtypeStruct((rows, 128), F32),
        ],
        compiler_params=params(),
        cost_estimate=pl.CostEstimate(
            flops=8 * rows * rows * width,
            bytes_accessed=10 * rows * width,
            transcendentals=4 * rows * rows,
        ),
        name="scores",
    )(q, *passages)


def take_rows(got_ref, place_ref, q_ref, f_ref):
    rows, width = q_ref.shape
    part = width // PARTS
    lane = iota((rows, got_ref.shape[0]), 1)
    main = one(lane == place_ref[:, 0:1])
    score = jnp.zeros((rows, 1), F32)
    for k in range(PARTS):
        at = slice(k * part, (k + 1) * part)
        fetched = dot(main, got_ref[:, at])
        fetched += dot(one(lane == place_ref[:, 1:2] + EXTRA * k), got_ref[:, width:])
        f_ref[:, at] = fetched.astype(BF16)
        score += jnp.sum(fetched * q_ref[:, at].astype(F32), axis=1, keepdims=True)
    return score


def unpack_kernel(got_ref, place_ref, q_ref, f_ref, hard_ref):
    hard_ref[...] = take_rows(got_ref, place_ref, q_ref, f_ref)


def unpack(got, place_cols, q):
    rows, width = q.shape[0], q.shape[1] // 2
    return pl.pallas_call(
        unpack_kernel,
        grid=(1,),
        in_specs=[whole(got.shape), whole((rows, 2)), pl.BlockSpec((rows, width), lambda i: (0, 0))],
        out_specs=[whole((rows, width)), whole((rows, 1))],
        out_shape=[
            jax.ShapeDtypeStruct((rows, width), BF16),
            jax.ShapeDtypeStruct((rows, 1), F32),
        ],
        compiler_params=params(),
        cost_estimate=pl.CostEstimate(
            flops=4 * got.shape[0] * rows * width,
            bytes_accessed=7 * rows * width,
            transcendentals=0,
        ),
        name="unpack",
    )(got, place_cols, q)


def soft_kernel(
    scale, got_ref, place_ref, q_ref, first_ref, stat_ref, f_ref, wcol_ref, norm_ref, vec_ref
):
    rows = q_ref.shape[0]
    score = (first_ref[...] + take_rows(got_ref, place_ref, q_ref, f_ref)) * scale
    top_in, total_in, diag = stat_ref[:, 0:1], stat_ref[:, 1:2], stat_ref[:, 2:3]
    top = jnp.maximum(top_in, score)
    norm = top + jnp.log(total_in * jnp.exp(top_in - top) + jnp.exp(score - top))
    weight = jnp.exp(score - norm).astype(BF16).astype(F32)
    wcol_ref[...] = weight
    norm_ref[...] = norm
    eye = iota((rows, rows), 0) == iota((rows, rows), 1)
    vec_ref[0:1, :] = jnp.sum(jnp.where(eye, norm, 0.0), axis=0, keepdims=True)
    vec_ref[1:2, :] = jnp.sum(jnp.where(eye, weight, 0.0), axis=0, keepdims=True)
    loss = jnp.sum(norm - diag, axis=0, keepdims=True)
    vec_ref[2:3, :] = jnp.broadcast_to(loss, (1, rows))
    vec_ref[3:8, :] = jnp.zeros((5, rows), F32)


def soft(scale, got, place_cols, q, first, stats):
    rows, width = q.shape[0], q.shape[1] // 2
    return pl.pallas_call(
        functools.partial(soft_kernel, scale),
        grid=(1,),
        in_specs=[
            whole(got.shape),
            whole((rows, 2)),
            pl.BlockSpec((rows, width), lambda i: (0, 1)),
            whole((rows, 1)),
            whole((rows, 128)),
        ],
        out_specs=[whole((rows, width)), whole((rows, 1)), whole((rows, 1)), whole((8, rows))],
        out_shape=[
            jax.ShapeDtypeStruct((rows, width), BF16),
            jax.ShapeDtypeStruct((rows, 1), F32),
            jax.ShapeDtypeStruct((rows, 1), F32),
            jax.ShapeDtypeStruct((8, rows), F32),
        ],
        compiler_params=params(),
        cost_estimate=pl.CostEstimate(
            flops=4 * got.shape[0] * rows * width,
            bytes_accessed=7 * rows * width,
            transcendentals=4 * rows,
        ),
        name="soft",
    )(got, place_cols, q, first, stats)


def stamp_kernel(place_ref, v0, v1, v2, v3, packed_ref, out_ref):
    n, rows = out_ref.shape[0], place_ref.shape[1]
    row, base = chunk_row((n, rows), 0)
    weight = v0[1:2, :]
    main = jnp.sum(jnp.where(row == place_ref[0:1, :], weight, 0.0), axis=1, keepdims=True)
    extra = jnp.sum(jnp.where(base == place_ref[1:2, :], weight, 0.0), axis=1, keepdims=True)
    loss = v0[2:3, 0:128] + v1[2:3, 0:128] + v2[2:3, 0:128] + v3[2:3, 0:128]
    high = loss.astype(BF16).astype(F32)
    mid = (loss - high).astype(BF16).astype(F32)
    low = loss - high - mid
    lane = iota((1, 128), 1)
    parts = jnp.where(lane == 2, high, jnp.where(lane == 3, mid, jnp.where(lane == 4, low, 0.0)))
    first = lax.rem(iota(out_ref.shape, 0), MAIN) == 0
    lane = iota(out_ref.shape, 1)
    notes = jnp.where(lane == 0, main, jnp.where(lane == 1, extra, jnp.where(first, parts, 0.0)))
    out_ref[...] = notes.astype(BF16)


def stamp(place_rows, vectors, packed):
    n, lanes = packed.shape
    return pl.pallas_call(
        stamp_kernel,
        grid=(1,),
        in_specs=[whole(place_rows.shape)]
        + [whole(v.shape) for v in vectors]
        + [pl.BlockSpec(memory_space=pl.ANY)],
        out_specs=pl.BlockSpec((n, 128), lambda i: (0, lanes // 128 - 1)),
        out_shape=jax.ShapeDtypeStruct((n, lanes), BF16),
        input_output_aliases={5: 0},
        compiler_params=params(60 * 1024 * 1024),
        name="stamp",
    )(place_rows, *vectors, packed)


def qgrad_kernel(s_ref, norm_ref, wcol_ref, p0, p1, p2, p3, f0, f1, out_ref, w):
    t = pl.program_id(0)
    rows = out_ref.shape[0]

    @pl.when(t == 0)
    def _():
        for j in range(4):
            v = jnp.exp(s_ref[:, j * rows : (j + 1) * rows] - norm_ref[...])
            if j == 0:
                eye = iota((rows, rows), 0) == iota((rows, rows), 1)
                v = jnp.where(eye, v - 1.0, v)
            w[:, j * rows : (j + 1) * rows] = v.astype(BF16)

    fetched = jnp.where(t < PARTS, f0[...].astype(F32), f1[...].astype(F32))
    acc = wcol_ref[...] * fetched
    for j, p in enumerate((p0, p1, p2, p3)):
        acc += dot(w[:, j * rows : (j + 1) * rows], p[...])
    out_ref[...] = acc


def qgrad(s, norm, wcol, passages, fetched):
    rows, width = passages[0].shape
    tile = width // (2 * PARTS)
    col = pl.BlockSpec((rows, tile), lambda t: (0, t))
    low = pl.BlockSpec((rows, tile), lambda t: (0, jnp.minimum(t, PARTS - 1)))
    high = pl.BlockSpec((rows, tile), lambda t: (0, jnp.maximum(t - PARTS, 0)))
    return pl.pallas_call(
        qgrad_kernel,
        grid=(2 * PARTS,),
        in_specs=[whole(s.shape), whole((rows, 1)), whole((rows, 1))] + [col] * 4 + [low, high],
        out_specs=col,
        out_shape=jax.ShapeDtypeStruct((rows, width), F32),
        scratch_shapes=[pltpu.VMEM((rows, 4 * rows), BF16)],
        compiler_params=params(),
        cost_estimate=pl.CostEstimate(
            flops=8 * rows * rows * width,
            bytes_accessed=14 * rows * width,
            transcendentals=4 * rows * rows,
        ),
        name="qgrad",
    )(s, norm, wcol, *passages, *fetched)


def pgrad_kernel(scale, p_ref, q0, q1, q2, q3, n0, n1, n2, n3, out_ref, wt):
    t = pl.program_id(0)
    rows = p_ref.shape[0]
    tile = out_ref.shape[1]
    queries = (q0, q1, q2, q3)

    @pl.when(t == 0)
    def _():
        for j, (q, norm) in enumerate(zip(queries, (n0, n1, n2, n3))):
            w = jnp.exp(dot_t(p_ref[...], q[...]) * scale - norm[0:1, :])
            if j == 0:
                eye = iota((rows, rows), 0) == iota((rows, rows), 1)
                w = jnp.where(eye, w - 1.0, w)
            wt[:, j * rows : (j + 1) * rows] = w.astype(BF16)

    at = pl.ds(pl.multiple_of(t * tile, tile), tile)
    acc = jnp.zeros(out_ref.shape, F32)
    for j, q in enumerate(queries):
        acc += dot(wt[:, j * rows : (j + 1) * rows], q[:, at])
    out_ref[...] = acc


def pgrad(scale, p, queries, norms):
    rows, width = p.shape
    tile = width // 8
    full = whole((rows, width))
    return pl.pallas_call(
        functools.partial(pgrad_kernel, scale),
        grid=(8,),
        in_specs=[full] * 5 + [whole((8, rows))] * 4,
        out_specs=pl.BlockSpec((rows, tile), lambda t: (0, t)),
        out_shape=jax.ShapeDtypeStruct((rows, width), F32),
        scratch_shapes=[pltpu.VMEM((rows, 4 * rows), BF16)],
        compiler_params=params(SMALL_BYTES),
        cost_estimate=pl.CostEstimate(
            flops=16 * rows * rows * width,
            bytes_accessed=14 * rows * width,
            transcendentals=4 * rows * rows,
        ),
        name="pgrad",
    )(p, *queries, *norms)


def finish_kernel(
    mean, half_ref, own_ref, pair_ref, main_ref, extra_ref, note_ref, part_ref, out_ref, mean_ref
):
    rows, width = out_ref.shape
    n, part = extra_ref.shape
    here = lax.div(iota((1, n), 1), n // 2) == half_ref[0]
    codes = jnp.where(here, own_ref[...], pair_ref[...])
    row = iota((rows, n), 0)
    hit = one(codes[0:1, :] == row)
    weight = note_ref[:, 0:1].astype(F32)
    late = (extra_ref[...].astype(F32) * note_ref[:, 1:2].astype(F32)).astype(BF16)
    for q in range(width // part):
        at = slice(q * part, (q + 1) * part)
        terms = (main_ref[:, at].astype(F32) * weight).astype(BF16)
        k = pl.program_id(0) * (width // part) + q
        acc = part_ref[:, at] + dot(hit, terms)
        out_ref[:, at] = acc + dot(one(codes[1:2, :] == row + rows * k), late)

    @pl.when(pl.program_id(0) == 0)
    def _():
        lane = iota(note_ref.shape, 1)
        parts = jnp.where((lane >= 2) & (lane <= 4), note_ref[...].astype(F32), 0.0)
        total = jnp.sum(parts, axis=0, keepdims=True)
        mean_ref[...] = jnp.sum(total, axis=1, keepdims=True) * mean


def finish(mean, half, own_rows, pair_rows, got, partial_grad):
    rows, width = partial_grad.shape
    n = got.shape[0]
    part = width // PARTS
    steps = 2
    col = pl.BlockSpec((rows, width // steps), lambda t: (0, t))
    return pl.pallas_call(
        functools.partial(finish_kernel, mean),
        grid=(steps,),
        in_specs=[
            pl.BlockSpec(memory_space=pltpu.SMEM),
            whole((2, n)),
            whole((2, n)),
            pl.BlockSpec((n, width // steps), lambda t: (0, t)),
            pl.BlockSpec((n, part), lambda t: (0, PARTS)),
            pl.BlockSpec((n, 128), lambda t: (0, (PARTS + 1) * part // 128)),
            col,
        ],
        out_specs=[col, whole((1, 1))],
        out_shape=[
            jax.ShapeDtypeStruct((rows, width), F32),
            jax.ShapeDtypeStruct((1, 1), F32),
        ],
        compiler_params=params(),
        cost_estimate=pl.CostEstimate(
            flops=4 * n * rows * width, bytes_accessed=11 * rows * width, transcendentals=0
        ),
        name="finish",
    )(half, own_rows, pair_rows, got, got, got, partial_grad)


def shards(queries, passages, hard_owner, hard_row):
    rows, width = queries.shape
    n_dp = lax.axis_size("dp")
    n_blk = lax.axis_size("blk")
    scale = 2.0 / math.sqrt(width)
    core = lax.rem(lax.axis_index("blk"), 2).astype(jnp.int32)
    half = lax.rem(lax.axis_index("dp") // 4, 2).astype(jnp.int32)
    half = lax.rem(half + core, 2).reshape(1)
    n = n_dp * MAIN

    def permute(x, table):
        return lax.ppermute(x, "blk", table)

    def exchange(x, groups):
        return lax.all_to_all(x, ("dp", "blk"), 0, 0, axis_index_groups=groups, tiled=True)

    p_low = passages[:, : width // 2]
    later, _ = lax.optimization_barrier((passages, p_low))
    p_halves = [p_low, later[:, width // 2 :]]
    pair_halves = [permute(p, PAIR) for p in p_halves]
    p_core = permute(passages, CORE)

    owner = hard_owner[:, 0]
    row = hard_row[:, 0]
    hits = (owner[:, None] == jnp.arange(n_dp, dtype=jnp.int32)[None, :]).astype(BF16)
    index = jnp.arange(rows, dtype=jnp.int32)
    before = (index[:, None] > index[None, :]).astype(BF16)
    slot = jnp.sum(dot(before, hits) * hits.astype(F32), axis=1).astype(jnp.int32)
    place = position(owner)
    chunk = jnp.where(core == 1, n_dp - 1 - place, place) * MAIN
    place_main = jnp.where(slot < MAIN, chunk + slot, -1)
    place_extra = jnp.where(slot < MAIN, -2 * MAIN, chunk + slot - MAIN)
    place_rows = jnp.stack([place_main, place_extra], axis=0)
    place_cols = jnp.stack([place_main, place_extra], axis=1)
    at = jnp.arange(n, dtype=jnp.int32)
    quarter = at % MAIN // EXTRA
    match = at[:, None] == place_main[None, :]
    code_main = jnp.sum(jnp.where(match, row[None, :] + 1, 0), axis=1) - 1
    match = (at - EXTRA * quarter)[:, None] == place_extra[None, :]
    code_extra = jnp.sum(jnp.where(match, row[None, :] + 1, 0), axis=1)
    code_extra = jnp.where(code_extra > 0, code_extra - 1 + rows * quarter, -1)
    codes = jnp.concatenate([code_main.reshape(n_dp, MAIN), code_extra.reshape(n_dp, MAIN)], axis=1)
    packed = pack(place_rows, queries, n)
    cut = 3 * rows // 4
    q_first = queries[:cut]
    asked, packed, q_first = lax.optimization_barrier(
        (exchange(codes, NEIGHBOURS), packed, q_first)
    )
    asked = asked.reshape(n_dp, 2, MAIN)
    asked_cols = asked.transpose(0, 2, 1).reshape(n, 2)
    asked_rows = asked.transpose(1, 0, 2).reshape(2, n)
    asked_pair = permute(asked_rows, PAIR)

    served = serve(half, asked_cols, p_halves[0], pair_halves[0])
    pair_high, _ = lax.optimization_barrier((pair_halves[1], served))
    served = [served, serve(half, asked_cols, p_halves[1], pair_high)]
    got = [exchange(x, NEIGHBOURS) for x in served]

    q_pair_first = permute(q_first, PAIR)
    q_core = permute(queries, CORE)

    p_pair = jnp.concatenate(pair_halves, axis=1)
    p_diag = permute(p_pair, CORE)
    passage_blocks = (passages, p_core, p_pair, p_diag)
    s, stats = scores(scale, queries, passage_blocks)
    fetched0, first = unpack(got[0], place_cols, queries)
    fetched1, wcol, norm, vectors = soft(scale, got[1], place_cols, queries, first, stats)

    vectors = (vectors, permute(vectors, CORE), permute(vectors, PAIR), permute(vectors, DIAG))

    q_last, *_ = lax.optimization_barrier((queries[cut:], *vectors[1:]))
    q_pair_last = permute(q_last, PAIR)
    sent = stamp(place_rows, vectors, packed)
    q_pair_first, sent = lax.optimization_barrier((q_pair_first, sent))
    q_pair = jnp.concatenate([q_pair_first, q_pair_last], axis=0)
    q_diag = permute(q_pair, CORE)
    terms = exchange(sent, COLUMNS)

    query_gradient = qgrad(s, norm, wcol, passage_blocks, (fetched0, fetched1))
    partial_grad = pgrad(scale, passages, (queries, q_core, q_pair, q_diag), vectors)
    mean = 1.0 / (rows * n_blk * n_dp)
    passage_gradient, loss = finish(mean, half, asked_rows, asked_pair, terms, partial_grad)
    return query_gradient, passage_gradient, loss.reshape(())


def solution(mesh):
    spec = P(("dp", "blk"), None)
    return jax.shard_map(
        shards,
        mesh=mesh,
        in_specs=(spec,) * 4,
        out_specs=(spec, spec, P()),
        check_vma=False,
    )
```
